32 devices in a mesh: dp: 8 (over z, x), tensor: 4 (over y, core).
Axes of the slice: x: 2, y: 2, z: 4, core: 2. Of those that a mesh axis runs over, the one named last changes fastest.
Arguments:
- tokens: bfloat16 [4096, 1024], P(('dp', 'tensor')), may hold values from -6 to 6
- seq_lengths: int32 [4], replicated, may hold values from 1 to 2048, 4096 in all
- norm_gain: float32 [1024], replicated, may hold values from 0.5 to 1.5
- mamba_in: bfloat16 [2, 1024, 1536], P(None, 'dp', 'tensor'), may hold values from -0.1875 to 0.1875
- dt_proj: bfloat16 [1024, 24], P('dp', 'tensor'), may hold values from -0.1875 to 0.1875
- bc_proj: bfloat16 [1024, 256], P('dp'), may hold values from -0.1875 to 0.1875
- conv_main: float32 [4, 1536], P(None, 'tensor'), may hold values from -3 to 3
- conv_shared: float32 [4, 256], replicated, may hold values from -3 to 3
- decay_log: float32 [24], P('tensor'), may hold values from -4 to 1.5
- dt_bias: float32 [24], P('tensor'), may hold values from -6 to -2
- skip_gain: float32 [24], P('tensor'), may hold values from 0.5 to 1.5
- gated_gain: float32 [1536], P('tensor'), may hold values from 0.5 to 1.5
- mamba_out: bfloat16 [1536, 1024], P('tensor', 'dp'), may hold values from -0.15625 to 0.15625
- query_proj: bfloat16 [1024, 512], P('dp', 'tensor'), may hold values from -0.1875 to 0.1875
- key_value_projection: bfloat16 [1024, 256], P('dp'), may hold values from -0.1875 to 0.1875
- attn_out: bfloat16 [512, 1024], P('tensor', 'dp'), may hold values from -4 to 4
- ffn_gain: float32 [1024], replicated, may hold values from 0.5 to 1.5
- ffn_in: bfloat16 [2, 1024, 2048], P(None, 'dp', 'tensor'), may hold values from -0.1875 to 0.1875
- ffn_down: bfloat16 [2048, 1024], P('tensor', 'dp'), may hold values from -0.125 to 0.125
- out_grad: bfloat16 [4096, 1024], P(('dp', 'tensor')), may hold values from -6 to 6
Outputs:
- layer_out: bfloat16 [4096, 1024], P(('dp', 'tensor'))
- grad_tokens: float32 [4096, 1024], P(('dp', 'tensor'))
- grad_norm_gain: float32 [1024], replicated
- grad_mamba_in: float32 [2, 1024, 1536], P(None, 'dp', 'tensor')
- grad_dt_proj: float32 [1024, 24], P('dp', 'tensor')
- grad_bc_proj: float32 [1024, 256], P('dp', 'tensor')
- grad_conv_main: float32 [4, 1536], P(None, 'tensor')
- grad_conv_shared: float32 [4, 256], replicated
- grad_decay_log: float32 [24], P('tensor')
- grad_dt_bias: float32 [24], P('tensor')
- grad_skip_gain: float32 [24], P('tensor')
- grad_gated_gain: float32 [1536], P('tensor')
- grad_mamba_out: float32 [1536, 1024], P('tensor', 'dp')
- grad_query_proj: float32 [1024, 512], P('dp', 'tensor')
- grad_kv_proj: float32 [1024, 256], P('dp', 'tensor')
- grad_attn_out: float32 [512, 1024], P('tensor', 'dp')
- grad_ffn_gain: float32 [1024], replicated
- grad_ffn_in: float32 [2, 1024, 2048], P(None, 'dp', 'tensor')
- grad_ffn_down: float32 [2048, 1024], P('tensor', 'dp')
The draws below stay inside these ranges and needn't reach their ends.
Inputs may be any that keep to these rules, and one draw needn't show every extreme that they name: `seq_lengths`: lengths of the 4 sequences packed in order; they sum to 4096 and the longest is 2048.
All inputs are finite; a program needn't handle non-finite values.
Results may differ from the reference program's by a relative error of at most 0.012.
The reference program's roundings to bfloat16 on the way (of `normed`, `mamba_norm`, `heads_out` and `hidden`) count: a program that leaves them out, or rounds other values in their place, can miss the bound.
Values may be sent and summed in bfloat16 or wider, within the bound.
A program may use at most 192 MiB of HBM per device.

```python
import math
import jax
import jax.numpy as jnp
import numpy as np
from jax import lax

MODEL_WIDTH = 1024
FF = 2048
HM = 24
P_SIZE = 64
NS = 128
KC = 4
QUERY_HEADS = 8
KEY_VALUE_HEADS = 2
HEAD_DIMENSION = 64
MAXLEN = 2048
DS = 1536
TOKENS = 4096
NSEQ = 4
QB = 512
SB = 128


def block_levels(own_key, extent, shards, low, top_value):
    factor_of = 1.0
    for dim, parts in shards:
        steps = jax.random.uniform(jax.random.fold_in(jax.random.fold_in(own_key, 6), dim), (parts,), jnp.float32, low / len(shards), top_value / len(shards))
        factor_of = factor_of * jnp.repeat(jnp.exp(steps), extent[dim] // parts).reshape((-1,) + (1,) * (len(extent) - 1 - dim))
    return factor_of


def split_up(number_of, total, bound, lean):
    portions = [(1 << 20) // math.isqrt(grade ** lean) + 1 for grade in range(2, number_of + 1)]
    spare, given = total - bound - (number_of - 1), [1] * (number_of - 1)
    while spare > 0:
        free = [i for i in range(number_of - 1) if given[i] < bound]
        pool, left = sum([portions[i] for i in free]), spare
        for i in free:
            more = min(bound - given[i], max(1, left * portions[i] // pool), spare)
            given[i] = given[i] + more
            spare = spare - more
    return np.array([bound] + given)


def uneven(rng, number_of, total, bound, slope):
    if number_of == 2:
        one = jax.random.randint(rng, (), max(1, total - bound), min(bound, total - 1) + 1)
        return jnp.stack([one, total - one])
    sizes = jnp.asarray(split_up(number_of, total, bound, slope), jnp.int32)
    couples = (number_of - 1) // 2
    source_of, taker = sizes[1:1 + 2 * couples:2], sizes[2:2 + 2 * couples:2]
    margin = jnp.minimum(source_of - 1, bound - taker)
    moved = jax.random.randint(jax.random.fold_in(rng, 1), (couples,), 0, 1 << 20) % (margin + 1)
    sizes = sizes.at[1:1 + 2 * couples:2].set(source_of - moved).at[2:2 + 2 * couples:2].set(taker + moved)
    return sizes[jax.random.permutation(jax.random.fold_in(rng, 2), number_of)]


def noise(own_key, extent, spread, most, shards=(), held_as=jnp.bfloat16):
    factor_of = block_levels(own_key, extent, shards, -0.22, 0.18) if shards else 1.0
    values = jax.random.normal(own_key, extent, jnp.float32) * spread * factor_of
    return jnp.minimum(jnp.maximum(values, -most), most).astype(held_as)


def setup_inputs(seed: int = 0) -> dict:
    key_list = jax.random.split(jax.random.key(seed), 21)
    return {
        "tokens": noise(key_list[0], (TOKENS, MODEL_WIDTH), 1.0, 6.0, ((0, 32),)),
        "seq_lengths": uneven(key_list[1], NSEQ, TOKENS, MAXLEN, 2).astype(jnp.int32),
        "norm_gain": jnp.clip(1.0 + 0.1 * jax.random.normal(key_list[2], (MODEL_WIDTH,), jnp.float32), 0.5, 1.5),
        "mamba_in": noise(key_list[3], (2, MODEL_WIDTH, DS), MODEL_WIDTH ** -0.5, 0.1875, ((1, 8), (2, 4))),
        "dt_proj": noise(key_list[4], (MODEL_WIDTH, HM), MODEL_WIDTH ** -0.5, 0.1875, ((0, 8), (1, 4))),
        "bc_proj": noise(key_list[5], (MODEL_WIDTH, 2 * NS), MODEL_WIDTH ** -0.5, 0.1875, ((0, 8),)),
        "conv_main": noise(key_list[6], (KC, DS), KC ** -0.5, 3.0, ((1, 4),), jnp.float32),
        "conv_shared": noise(key_list[7], (KC, 2 * NS), KC ** -0.5, 3.0, (), jnp.float32),
        "decay_log": jnp.clip(-4.0 + 5.5 * jax.random.uniform(key_list[8], (HM,), jnp.float32) ** block_levels(key_list[8], (HM,), ((0, 4),), -0.2, 0.2), -4.0, 1.5),
        "dt_bias": jnp.clip(-6.0 + 4.0 * jax.random.uniform(key_list[9], (HM,), jnp.float32) ** block_levels(key_list[9], (HM,), ((0, 4),), -0.2, 0.2), -6.0, -2.0),
        "skip_gain": jnp.clip(0.5 + 1.0 * jax.random.uniform(key_list[10], (HM,), jnp.float32) ** block_levels(key_list[10], (HM,), ((0, 4),), -0.2, 0.2), 0.5, 1.5),
        "gated_gain": jnp.clip(1.0 + 0.1 * jax.random.normal(key_list[11], (DS,), jnp.float32), 0.5, 1.5),
        "mamba_out": noise(key_list[12], (DS, MODEL_WIDTH), DS ** -0.5, 0.15625, ((0, 4), (1, 8))),
        "query_proj": noise(key_list[13], (MODEL_WIDTH, QUERY_HEADS * HEAD_DIMENSION), MODEL_WIDTH ** -0.5, 0.1875, ((0, 8), (1, 4))),
        "key_value_projection": noise(key_list[14], (MODEL_WIDTH, 2 * KEY_VALUE_HEADS * HEAD_DIMENSION), MODEL_WIDTH ** -0.5, 0.1875, ((0, 8),)),
        "attn_out": noise(key_list[15], (QUERY_HEADS * HEAD_DIMENSION, MODEL_WIDTH), (max(1, QUERY_HEADS * HEAD_DIMENSION // 256)) ** -0.5, 4.0, ((0, 4), (1, 8))),
        "ffn_gain": jnp.clip(1.0 + 0.1 * jax.random.normal(key_list[16], (MODEL_WIDTH,), jnp.float32), 0.5, 1.5),
        "ffn_in": noise(key_list[17], (2, MODEL_WIDTH, FF), MODEL_WIDTH ** -0.5, 0.1875, ((1, 8), (2, 4))),
        "ffn_down": noise(key_list[18], (FF, MODEL_WIDTH), FF ** -0.5, 0.125, ((0, 4), (1, 8))),
        "out_grad": noise(key_list[19], (TOKENS, MODEL_WIDTH), 1.0, 6.0, ((0, 32),)),
    }


@jax.custom_vjp
def lower_bound(v):
    return lax.optimization_barrier(v.astype(jnp.bfloat16)).astype(jnp.float32)

@jax.custom_vjp
def low_back(v):
    return v

def low_keep(v):
    return (lower_bound(v), None)

def low_pass(kept, grad):
    return (grad,)

def back_keep(v):
    return (v, None)

def back_low(kept, grad):
    return (lower_bound(grad),)
lower_bound.defvjp(low_keep, low_pass)
low_back.defvjp(back_keep, back_low)
HIGHEST = lax.Precision.HIGHEST
EPSILON = 1e-05
ROTARY_BASE = 100000000000.0
MASKED = -1e+30

def layout(lengths, first, length):
    starts = (jnp.cumsum(lengths) - lengths).astype(jnp.int32)
    token_ids = (first + jnp.arange(length, dtype=jnp.int32)).astype(jnp.int32)
    segment = lax.optimization_barrier(jnp.sum((starts[None, :] <= token_ids[:, None]).astype(jnp.int32), axis=1)).astype(jnp.int32) - 1
    owner = jnp.arange(starts.shape[0], dtype=jnp.int32)[None, :] == segment[:, None]
    position = (token_ids - lax.optimization_barrier(jnp.sum(jnp.where(owner, starts[None, :], 0), axis=1))).astype(jnp.int32)
    return (segment, position)

def rms_rows(value_rows, scale):
    return value_rows * lax.rsqrt(lax.optimization_barrier(jnp.mean(value_rows * value_rows, axis=-1, keepdims=True)) + EPSILON) * scale

def softplus(value_rows):
    return jnp.maximum(value_rows, 0.0) + jnp.log1p(jnp.exp(-jnp.abs(value_rows)))

def silu(value_rows):
    return value_rows * lax.logistic(value_rows)

def rotary(value_rows, position, sign):
    half = value_rows.shape[-1] // 2
    freqs = ROTARY_BASE ** (-2.0 * jnp.arange(half, dtype=jnp.float32) / value_rows.shape[-1])
    angle = position.astype(jnp.float32)[:, None] * freqs[None, :]
    cosine = jnp.cos(angle)[:, None, :]
    sine = sign * jnp.sin(angle)[:, None, :]
    first_half = value_rows[..., :half]
    second_half = value_rows[..., half:]
    return jnp.concatenate([first_half * cosine - second_half * sine, second_half * cosine + first_half * sine], axis=-1)

def causal_conv(extended, weight, seg_ext, length):
    lead = weight.shape[0] - 1
    result = weight[0] * extended[lead:]
    for offset in range(1, weight.shape[0]):
        moved = extended[lead - offset:lead - offset + length]
        same = seg_ext[lead - offset:lead - offset + length] == seg_ext[lead:]
        result = result + weight[offset] * jnp.where(same[:, None], moved, 0.0)
    return result

def ssd_block(carry_state, inputs):
    inner, shared_b, shared_c, step_sizes, log_rates, segment, before = inputs
    running = jnp.cumsum(log_rates, axis=0)
    length = step_sizes.shape[0]
    row_ids = jnp.arange(length, dtype=jnp.int32)
    allowed = (segment[:, None] == segment[None, :]) & (row_ids[:, None] >= row_ids[None, :])
    log_gaps = running[:, None, :] - running[None, :, :]
    decays = jnp.exp(jnp.where(allowed[:, :, None], log_gaps, MASKED))
    intersection = jnp.dot(shared_c, shared_b.T, precision=HIGHEST)
    weights = decays * intersection[:, :, None] * step_sizes[None, :, :]
    output = jnp.einsum('ijh,jhp->ihp', weights, inner, precision=HIGHEST)
    carried = jnp.exp(running) * (segment == before)[:, None]
    output = output + carried[:, :, None] * jnp.einsum('hpn,in->ihp', carry_state, shared_c, precision=HIGHEST)
    tail_weight = jnp.exp(running[-1][None, :] - running) * (segment == segment[-1])[:, None] * step_sizes
    keep_rate = jnp.exp(running[-1]) * (segment[-1] == before)
    carry_state = keep_rate[:, None, None] * carry_state + jnp.einsum('jh,jhp,jn->hpn', tail_weight, inner, shared_b, precision=HIGHEST)
    return (carry_state, output)

def ssd_whole(inner, shared_b, shared_c, step_sizes, log_rates, segment, block):
    total_count = step_sizes.shape[0]
    blocks = total_count // block
    before_all = jnp.concatenate([jnp.full((1,), -1, jnp.int32), segment[:-1]])
    pieces = (inner.reshape(blocks, block, inner.shape[1], inner.shape[2]), shared_b.reshape(blocks, block, -1), shared_c.reshape(blocks, block, -1), step_sizes.reshape(blocks, block, -1), log_rates.reshape(blocks, block, -1), segment.reshape(blocks, block), before_all.reshape(blocks, block)[:, 0])
    start_state = jnp.zeros((inner.shape[1], inner.shape[2], shared_b.shape[1]), jnp.float32)
    final_state, output = lax.scan(jax.checkpoint(ssd_block), start_state, pieces)
    return output.reshape(inner.shape)

def attention(queries, key_rows, value_rows, segment, block, window):
    total_count = queries.shape[0]
    kv_heads = key_rows.shape[1]
    groups = queries.shape[1] // kv_heads
    head_size = key_rows.shape[2]
    pad_keys = jnp.concatenate([jnp.zeros((window, kv_heads, head_size), jnp.float32), key_rows])
    pad_values = jnp.concatenate([jnp.zeros((window, kv_heads, head_size), jnp.float32), value_rows])
    pad_seg = jnp.concatenate([jnp.full((window,), -1, jnp.int32), segment])
    scale = head_size ** (-0.5)

    def one_block(start):
        query_blk = lax.dynamic_slice_in_dim(queries, start, block, 0).reshape(block, kv_heads, groups, head_size)
        key_blk = lax.dynamic_slice_in_dim(pad_keys, start, block + window, 0)
        value_blk = lax.dynamic_slice_in_dim(pad_values, start, block + window, 0)
        seg_keys = lax.dynamic_slice_in_dim(pad_seg, start, block + window, 0)
        seg_rows = lax.dynamic_slice_in_dim(segment, start, block, 0)
        row_index = start + jnp.arange(block, dtype=jnp.int32)
        key_index = start - window + jnp.arange(block + window, dtype=jnp.int32)
        allowed = (seg_keys[None, :] == seg_rows[:, None]) & (key_index[None, :] <= row_index[:, None])
        scores = low_back(scale * jnp.einsum('qcgd,kcd->cgqk', query_blk, key_blk, precision=HIGHEST))
        scores = jnp.where(allowed[None, None], scores, MASKED)
        row_max = lax.optimization_barrier(jnp.max(scores, axis=-1, keepdims=True))
        shifted = jnp.exp(scores - row_max)
        probs = lower_bound(shifted / lax.optimization_barrier(jnp.sum(shifted, axis=-1, keepdims=True)))
        return jnp.einsum('cgqk,kcd->qcgd', probs, value_blk, precision=HIGHEST).reshape(block, -1)
    starts = (jnp.arange(total_count // block, dtype=jnp.int32) * block).astype(jnp.int32)
    return lax.map(jax.checkpoint(one_block), starts).reshape(total_count, -1)

def forward(tokens, norm_gain, mamba_in, dt_proj, bc_proj, conv_main, conv_shared, decay_log, dt_bias, skip_gain, gated_gain, mamba_out, query_proj, key_value_projection, attn_out, ffn_gain, ffn_in, ffn_down, segment, position):
    total_count = tokens.shape[0]
    normed = lower_bound(rms_rows(tokens, norm_gain))
    gate_z = lower_bound(low_back(jnp.dot(normed, mamba_in[0], precision=HIGHEST)))
    mixer_x = lower_bound(low_back(jnp.dot(normed, mamba_in[1], precision=HIGHEST)))
    shared_bc = lower_bound(low_back(jnp.dot(normed, bc_proj, precision=HIGHEST)))
    step_raw = low_back(jnp.dot(normed, dt_proj, precision=HIGHEST))
    lead = KC - 1
    seg_ext = jnp.concatenate([jnp.full((lead,), -1, jnp.int32), segment])
    conv_x = silu(causal_conv(jnp.concatenate([jnp.zeros((lead, DS), jnp.float32), mixer_x]), conv_main, seg_ext, total_count))
    conv_bc = silu(causal_conv(jnp.concatenate([jnp.zeros((lead, 2 * NS), jnp.float32), shared_bc]), conv_shared, seg_ext, total_count))
    step_sizes = softplus(step_raw + dt_bias)
    log_rates = -jnp.exp(decay_log) * step_sizes
    inner = conv_x.reshape(total_count, HM, P_SIZE)
    states_out = ssd_whole(inner, conv_bc[:, :NS], conv_bc[:, NS:], step_sizes, log_rates, segment, SB)
    result = (states_out + skip_gain[None, :, None] * inner).reshape(total_count, DS)
    gated = result * silu(gate_z)
    mamba_norm = lower_bound(rms_rows(gated, gated_gain))
    queries = low_back(jnp.dot(normed, query_proj, precision=HIGHEST)).reshape(total_count, QUERY_HEADS, HEAD_DIMENSION)
    key_value_unnormed = low_back(jnp.dot(normed, key_value_projection, precision=HIGHEST))
    key_rows = key_value_unnormed[:, :KEY_VALUE_HEADS * HEAD_DIMENSION].reshape(total_count, KEY_VALUE_HEADS, HEAD_DIMENSION)
    value_rows = lower_bound(key_value_unnormed[:, KEY_VALUE_HEADS * HEAD_DIMENSION:].reshape(total_count, KEY_VALUE_HEADS, HEAD_DIMENSION))
    queries = lower_bound(rotary(queries, position, 1.0))
    key_rows = lower_bound(rotary(key_rows, position, 1.0))
    window = (MAXLEN - 1 + QB - 1) // QB * QB
    heads_out = lower_bound(low_back(attention(queries, key_rows, value_rows, segment, QB, window)))
    mixed = low_back(jnp.dot(mamba_norm, mamba_out, precision=HIGHEST) + jnp.dot(heads_out, attn_out, precision=HIGHEST))
    middle = tokens + mixed
    normed_two = lower_bound(rms_rows(middle, ffn_gain))
    gate_up = jnp.einsum('td,sdf->stf', normed_two, ffn_in, precision=HIGHEST)
    gate_val = lower_bound(low_back(gate_up[0]))
    up_val = lower_bound(low_back(gate_up[1]))
    hidden = lower_bound(silu(gate_val) * up_val)
    return middle + jnp.dot(hidden, ffn_down, precision=HIGHEST)

def reference(tokens, seq_lengths, norm_gain, mamba_in, dt_proj, bc_proj, conv_main, conv_shared, decay_log, dt_bias, skip_gain, gated_gain, mamba_out, query_proj, key_value_projection, attn_out, ffn_gain, ffn_in, ffn_down, out_grad):
    segment, position = layout(seq_lengths, 0, tokens.shape[0])
    floats = tuple((array.astype(jnp.float32) for array in (tokens, norm_gain, mamba_in, dt_proj, bc_proj, conv_main, conv_shared, decay_log, dt_bias, skip_gain, gated_gain, mamba_out, query_proj, key_value_projection, attn_out, ffn_gain, ffn_in, ffn_down)))
    output, pull = jax.vjp(lambda *params: forward(*params, segment, position), *floats)
    grads = pull(out_grad.astype(jnp.float32))
    return (output.astype(jnp.bfloat16), grads[0], grads[1], grads[2], grads[3], grads[4], grads[5], grads[6], grads[7], grads[8], grads[9], grads[10], grads[11], grads[12], grads[13], grads[14], grads[15], grads[16], grads[17])
```

```python
from functools import partial

import jax
import jax.numpy as jnp
from jax import lax
from jax.sharding import PartitionSpec as P

QUERY_HEADS = 8
KEY_VALUE_HEADS = 2
HEAD_DIMENSION = 64
MAXLEN = 2048
DS = 1536


HIGHEST = lax.Precision.HIGHEST
EPSILON = 1e-05
ROTARY_BASE = 100000000000.0
MASKED = -1e30


def prefix(part, axis, combine, identity, reverse):
    count = lax.axis_size(axis)
    place = lax.axis_index(axis)
    ahead = count - 1 - place if reverse else place
    gathered = jax.tree.map(lambda a: lax.all_gather(a, axis), part)
    state = jax.tree.map(lambda a, e: jnp.zeros_like(a) + jnp.asarray(e, a.dtype), part, identity)

    def one(step, state):
        source = count - 1 - step if reverse else step
        return combine(
            state, jax.tree.map(lambda a: lax.dynamic_index_in_dim(a, source, 0, False), gathered)
        )

    return lax.fori_loop(0, ahead, one, state)


def passed_along(value, axis, steps):
    count = lax.axis_size(axis)
    leading, last = (max(0, -steps), min(count, count - steps))
    return lax.ppermute(value, axis, [(source, source + steps) for source in range(leading, last)])


def layout(lengths, first, length):
    starts = jnp.cumsum(lengths) - lengths
    token_ids = first + jnp.arange(length, dtype=jnp.int32)
    segment = jnp.sum((starts[None, :] <= token_ids[:, None]).astype(jnp.int32), axis=1) - 1
    owner = jnp.arange(starts.shape[0], dtype=jnp.int32)[None, :] == segment[:, None]
    position = token_ids - jnp.sum(jnp.where(owner, starts[None, :], 0), axis=1)
    return (segment, position)


def rms_rows(value_rows, scale):
    return (
        value_rows
        * lax.rsqrt(jnp.mean(value_rows * value_rows, axis=-1, keepdims=True) + EPSILON)
        * scale
    )


def softplus(value_rows):
    return jnp.maximum(value_rows, 0.0) + jnp.log1p(jnp.exp(-jnp.abs(value_rows)))


def silu(value_rows):
    return value_rows * lax.logistic(value_rows)


def rotary(value_rows, position, sign):
    half = value_rows.shape[-1] // 2
    freqs = ROTARY_BASE ** (-2.0 * jnp.arange(half, dtype=jnp.float32) / value_rows.shape[-1])
    angle = position.astype(jnp.float32)[:, None] * freqs[None, :]
    cosine = jnp.cos(angle)[:, None, :]
    sine = sign * jnp.sin(angle)[:, None, :]
    first_half = value_rows[..., :half]
    second_half = value_rows[..., half:]
    return jnp.concatenate(
        [first_half * cosine - second_half * sine, second_half * cosine + first_half * sine],
        axis=-1,
    )


def causal_conv(extended, weight, seg_ext, length):
    lead = weight.shape[0] - 1
    result = weight[0] * extended[lead:]
    for offset in range(1, weight.shape[0]):
        moved = extended[lead - offset : lead - offset + length]
        same = seg_ext[lead - offset : lead - offset + length] == seg_ext[lead:]
        result = result + weight[offset] * jnp.where(same[:, None], moved, 0.0)
    return result


def ssd_block(carry_state, inputs):
    inner, shared_b, shared_c, step_sizes, log_rates, segment, before = inputs
    running = jnp.cumsum(log_rates, axis=0)
    length = step_sizes.shape[0]
    row_ids = jnp.arange(length, dtype=jnp.int32)
    allowed = (segment[:, None] == segment[None, :]) & (row_ids[:, None] >= row_ids[None, :])
    log_gaps = running[:, None, :] - running[None, :, :]
    decays = jnp.exp(jnp.where(allowed[:, :, None], log_gaps, MASKED))
    intersection = jnp.dot(shared_c, shared_b.T, precision=HIGHEST)
    weights = decays * intersection[:, :, None] * step_sizes[None, :, :]
    output = jnp.einsum("ijh,jhp->ihp", weights, inner, precision=HIGHEST)
    carried = jnp.exp(running) * (segment == before)[:, None]
    output = output + carried[:, :, None] * jnp.einsum(
        "hpn,in->ihp", carry_state, shared_c, precision=HIGHEST
    )
    tail_weight = (
        jnp.exp(running[-1][None, :] - running) * (segment == segment[-1])[:, None] * step_sizes
    )
    keep_rate = jnp.exp(running[-1]) * (segment[-1] == before)
    carry_state = keep_rate[:, None, None] * carry_state + jnp.einsum(
        "jh,jhp,jn->hpn", tail_weight, inner, shared_b, precision=HIGHEST
    )
    return (carry_state, output)


def mamba_inputs(
    mixer_ext, shared_ext, step_raw, conv_main, conv_shared, decay_log, dt_bias, seg_ext, heads
):
    length = step_raw.shape[0]
    conv_x = silu(causal_conv(mixer_ext, conv_main, seg_ext, length))
    conv_bc = silu(causal_conv(shared_ext, conv_shared, seg_ext, length))
    states = conv_bc.shape[1] // 2
    step_sizes = softplus(step_raw + dt_bias)
    log_rates = -jnp.exp(decay_log) * step_sizes
    return (
        conv_x.reshape(length, heads, -1),
        conv_bc[:, :states],
        conv_bc[:, states:],
        step_sizes,
        log_rates,
    )


def local_scan(inner, shared_b, shared_c, step_sizes, log_rates, segment, before, block):
    length = step_sizes.shape[0]
    blocks = length // block
    block_before = jnp.concatenate([before[None], segment[:-1]])
    pieces = (
        inner.reshape(blocks, block, inner.shape[1], inner.shape[2]),
        shared_b.reshape(blocks, block, -1),
        shared_c.reshape(blocks, block, -1),
        step_sizes.reshape(blocks, block, -1),
        log_rates.reshape(blocks, block, -1),
        segment.reshape(blocks, block),
        block_before.reshape(blocks, block)[:, 0],
    )
    start_state = jnp.zeros((inner.shape[1], inner.shape[2], shared_b.shape[1]), jnp.float32)
    final_state, output = lax.scan(jax.checkpoint(ssd_block), start_state, pieces)
    carry_rate = jnp.exp(jnp.sum(log_rates, axis=0)) * (segment[-1] == before)
    return (output.reshape(inner.shape), carry_rate, final_state)


def mamba_output(
    local_out, state_in, inner, shared_c, log_rates, skip_gain, gate_z, segment, before
):
    running = jnp.cumsum(log_rates, axis=0)
    carried = jnp.exp(running) * (segment == before)[:, None]
    result = local_out + carried[:, :, None] * jnp.einsum(
        "hpn,in->ihp", state_in, shared_c, precision=HIGHEST
    )
    result = result + skip_gain[None, :, None] * inner
    gated = result.reshape(gate_z.shape) * silu(gate_z)
    return (gated, jnp.sum(gated * gated, axis=1))


def gated_norm(gated, squares, gated_gain):
    return gated * lax.rsqrt(squares[:, None] / DS + EPSILON) * gated_gain


def attend_block(query_blk, key_rows, value_rows, allowed, scale):
    scores = (
        jnp.einsum("qgd,kd->gqk", query_blk, key_rows, preferred_element_type=jnp.float32) * scale
    )
    scores = jnp.where(allowed[None], scores, MASKED)
    row_max = jnp.max(scores, axis=-1, keepdims=True)
    shifted = jnp.exp(scores - row_max)
    row_total = jnp.sum(shifted, axis=-1, keepdims=True)
    probs = (shifted / row_total).astype(jnp.bfloat16)
    output = jnp.einsum("gqk,kd->qgd", probs, value_rows, preferred_element_type=jnp.float32)
    return (output, (row_max + jnp.log(row_total))[..., 0])


def attend_back(query_blk, key_rows, value_rows, allowed, scale, row_lse, grad_out):
    scores = (
        jnp.einsum("qgd,kd->gqk", query_blk, key_rows, preferred_element_type=jnp.float32) * scale
    )
    scores = jnp.where(allowed[None], scores, MASKED)
    probs = jnp.exp(scores - row_lse[..., None])
    grad_values = jnp.einsum(
        "gqk,qgd->kd", probs.astype(jnp.bfloat16), grad_out, preferred_element_type=jnp.float32
    )
    grad_probs = jnp.einsum("qgd,kd->gqk", grad_out, value_rows, preferred_element_type=jnp.float32)
    inner_sum = jnp.sum(grad_probs * probs, axis=-1, keepdims=True)
    grad_scores = (probs * (grad_probs - inner_sum)).astype(jnp.bfloat16) * scale
    grad_query = jnp.einsum(
        "gqk,kd->qgd", grad_scores, key_rows, preferred_element_type=jnp.float32
    )
    grad_keys = jnp.einsum(
        "gqk,qgd->kd", grad_scores, query_blk, preferred_element_type=jnp.float32
    )
    return (grad_query, grad_keys, grad_values)


def per_device(
    tokens,
    seq_lengths,
    norm_gain,
    mamba_in,
    dt_proj,
    bc_proj,
    conv_main,
    conv_shared,
    decay_log,
    dt_bias,
    skip_gain,
    gated_gain,
    mamba_out,
    query_proj,
    key_value_projection,
    attn_out,
    ffn_gain,
    ffn_in,
    ffn_down,
    out_grad,
):
    tensor_size = lax.axis_size("tensor")
    tensor_position = lax.axis_index("tensor")
    group_at = lax.axis_index("dp")
    own_rows = tokens.shape[0]
    group_rows = own_rows * tensor_size
    first_row = group_at * group_rows
    lead = conv_main.shape[0] - 1
    hops = (MAXLEN + group_rows - 2) // group_rows
    scan_block = min(128, group_rows)
    local_heads = decay_log.shape[0]
    query_head_rows = query_proj.shape[1] // HEAD_DIMENSION
    key_value_head = tensor_position * query_head_rows // (QUERY_HEADS // KEY_VALUE_HEADS)
    scale = HEAD_DIMENSION ** (-0.5)
    segment, position = layout(seq_lengths, first_row, group_rows)
    before = layout(seq_lengths, first_row - 1, 1)[0][0]
    seg_ext = layout(seq_lengths, first_row - lead, group_rows + lead)[0]
    key_first = first_row - hops * group_rows
    key_seg = layout(seq_lengths, key_first, (hops + 1) * group_rows)[0]
    key_index = key_first + jnp.arange((hops + 1) * group_rows, dtype=jnp.int32)
    query_index = first_row + jnp.arange(group_rows, dtype=jnp.int32)

    def spread(own_part):
        return lax.all_gather(own_part, "tensor", axis=0, tiled=True)

    def summed_rows(group_part):
        return lax.psum_scatter(group_part, "tensor", scatter_dimension=0, tiled=True)

    def tensor_total(row_values):
        return lax.psum(row_values, "tensor")

    def pass_states(rates, states, step):

        def link_pair(earlier, later):
            return (earlier[0] * later[0], later[0][:, None, None] * earlier[1] + later[1])

        return prefix(
            (rates, states),
            "dp",
            link_pair,
            (jnp.ones_like(rates), jnp.zeros_like(states)),
            step < 0,
        )[1]

    def block_mask():
        return (key_seg[None, :] == segment[:, None]) & (key_index[None, :] <= query_index[:, None])

    def pack(parts):
        return jnp.concatenate(parts, axis=1)

    def unpack(packed, widths):
        pieces, at = [], 0
        for width in widths:
            pieces.append(packed[:, at : at + width])
            at += width
        return pieces

    first_parts = (
        mamba_in[0],
        mamba_in[1],
        bc_proj,
        key_value_projection,
        query_proj,
        dt_proj,
    )
    second_parts = (mamba_out.T, attn_out.T, ffn_down.T, ffn_in[0], ffn_in[1])
    first_whole = lax.all_gather(pack(first_parts), "dp", axis=0, tiled=True)
    second_whole = lax.all_gather(pack(second_parts), "dp", axis=0, tiled=True)
    full_mamba_gate, full_mamba_mixer, full_bc, gathered_key_value, full_query, full_dt = unpack(
        first_whole, [part.shape[1] for part in first_parts]
    )
    full_mamba_in = jnp.stack([full_mamba_gate, full_mamba_mixer])
    out_t, attn_t, down_t, full_ffn_gate, full_ffn_up = unpack(
        second_whole, [part.shape[1] for part in second_parts]
    )
    full_mamba_out, full_attn_out, full_ffn_down = out_t.T, attn_t.T, down_t.T
    full_ffn_in = jnp.stack([full_ffn_gate, full_ffn_up])
    normed_own, pull_norm_one = jax.vjp(rms_rows, tokens.astype(jnp.float32), norm_gain)
    normed = spread(normed_own.astype(jnp.bfloat16))
    projected = jnp.einsum(
        "td,sdc->stc", normed, full_mamba_in, preferred_element_type=jnp.float32
    ).astype(jnp.bfloat16)
    gate_z = projected[0]
    mixer_x = projected[1]
    shared_bc = jnp.dot(normed, full_bc, preferred_element_type=jnp.float32).astype(jnp.bfloat16)
    step_raw = jnp.dot(normed, full_dt, preferred_element_type=jnp.float32)
    query_raw = jnp.dot(normed, full_query, preferred_element_type=jnp.float32)
    kv_cols = jnp.concatenate(
        [
            lax.dynamic_slice_in_dim(
                gathered_key_value, key_value_head * HEAD_DIMENSION, HEAD_DIMENSION, 1
            ),
            lax.dynamic_slice_in_dim(
                gathered_key_value,
                (KEY_VALUE_HEADS + key_value_head) * HEAD_DIMENSION,
                HEAD_DIMENSION,
                1,
            ),
        ],
        axis=1,
    )
    key_value_unnormed = jnp.dot(normed, kv_cols, preferred_element_type=jnp.float32)
    queries = rotary(
        query_raw.reshape(group_rows, query_head_rows, HEAD_DIMENSION), position, 1.0
    ).astype(jnp.bfloat16)
    key_rows = rotary(key_value_unnormed[:, None, :HEAD_DIMENSION], position, 1.0)[:, 0].astype(
        jnp.bfloat16
    )
    value_rows = key_value_unnormed[:, HEAD_DIMENSION:].astype(jnp.bfloat16)
    tails = passed_along((mixer_x[-lead:], shared_bc[-lead:]), "dp", 1)
    mixer_ext = jnp.concatenate([tails[0], mixer_x]).astype(jnp.float32)
    shared_ext = jnp.concatenate([tails[1], shared_bc]).astype(jnp.float32)
    prepared, pull_inputs = jax.vjp(
        partial(mamba_inputs, seg_ext=seg_ext, heads=local_heads),
        mixer_ext,
        shared_ext,
        step_raw,
        conv_main,
        conv_shared,
        decay_log,
        dt_bias,
    )
    inner, shared_b, shared_c, step_sizes, log_rates = prepared
    scanned, pull_scan = jax.vjp(
        partial(local_scan, segment=segment, before=before, block=scan_block),
        inner,
        shared_b,
        shared_c,
        step_sizes,
        log_rates,
    )
    local_out, carry_rate, final_state = scanned
    state_in = pass_states(carry_rate, final_state, 1)
    after, pull_after = jax.vjp(
        partial(mamba_output, segment=segment, before=before),
        local_out,
        state_in,
        inner,
        shared_c,
        log_rates,
        skip_gain,
        gate_z.astype(jnp.float32),
    )
    gated, own_squares = after
    squares = tensor_total(own_squares)
    mamba_norm, pull_gated = jax.vjp(gated_norm, gated, squares, gated_gain)
    mamba_low = mamba_norm.astype(jnp.bfloat16)
    own_pair = jnp.concatenate([key_rows, value_rows], axis=1)
    arrived = [passed_along(own_pair, "dp", distance) for distance in range(hops, 0, -1)]
    all_pairs = jnp.concatenate(arrived + [own_pair])
    all_keys = all_pairs[:, :HEAD_DIMENSION]
    all_values = all_pairs[:, HEAD_DIMENSION:]
    output, row_lse = attend_block(queries, all_keys, all_values, block_mask(), scale)
    heads_out = output.reshape(group_rows, query_head_rows * HEAD_DIMENSION).astype(jnp.bfloat16)
    mixed_part = jnp.dot(mamba_low, full_mamba_out, preferred_element_type=jnp.float32)
    mixed_part = mixed_part + jnp.dot(heads_out, full_attn_out, preferred_element_type=jnp.float32)
    middle = tokens.astype(jnp.float32) + summed_rows(mixed_part)
    normed_two_own, pull_norm_two = jax.vjp(rms_rows, middle, ffn_gain)
    normed_two = spread(normed_two_own.astype(jnp.bfloat16))
    gate_up = jnp.einsum(
        "td,sdf->stf", normed_two, full_ffn_in, preferred_element_type=jnp.float32
    ).astype(jnp.bfloat16)
    gate_val = gate_up[0].astype(jnp.float32)
    up_val = gate_up[1].astype(jnp.float32)
    hidden = (silu(gate_val) * up_val).astype(jnp.bfloat16)
    layer_out = (
        middle + summed_rows(jnp.dot(hidden, full_ffn_down, preferred_element_type=jnp.float32))
    ).astype(jnp.bfloat16)
    grad_full = spread(out_grad)
    grad_ffn_down = jnp.einsum("td,tf->df", grad_full, hidden, preferred_element_type=jnp.float32)
    grad_hidden = jnp.einsum(
        "td,fd->tf", grad_full, full_ffn_down, preferred_element_type=jnp.float32
    )
    sigma = lax.logistic(gate_val)
    grad_gate_up = jnp.stack(
        [
            grad_hidden * up_val * sigma * (1.0 + gate_val * (1.0 - sigma)),
            grad_hidden * gate_val * sigma,
        ]
    ).astype(jnp.bfloat16)
    grad_ffn_in = jnp.einsum(
        "td,stf->sdf", normed_two, grad_gate_up, preferred_element_type=jnp.float32
    )
    grad_normed_two = summed_rows(
        jnp.einsum("stf,sdf->td", grad_gate_up, full_ffn_in, preferred_element_type=jnp.float32)
    )
    grad_middle_norm, grad_ffn_gain = pull_norm_two(grad_normed_two)
    grad_middle = out_grad.astype(jnp.float32) + grad_middle_norm
    grad_mixed = spread(grad_middle.astype(jnp.bfloat16))
    grad_mamba_out = jnp.einsum(
        "td,tc->dc", grad_mixed, mamba_low, preferred_element_type=jnp.float32
    )
    grad_attn_out = jnp.einsum(
        "td,tc->dc", grad_mixed, heads_out, preferred_element_type=jnp.float32
    )
    grad_mamba_norm = jnp.einsum(
        "td,cd->tc", grad_mixed, full_mamba_out, preferred_element_type=jnp.float32
    )
    grad_heads = jnp.einsum(
        "td,cd->tc", grad_mixed, full_attn_out, preferred_element_type=jnp.float32
    )
    grad_heads = grad_heads.astype(jnp.bfloat16).reshape(
        group_rows, query_head_rows, HEAD_DIMENSION
    )
    grad_gated, grad_squares, grad_gated_gain = pull_gated(grad_mamba_norm)
    grad_own_squares = tensor_total(grad_squares)
    after_grads = pull_after((grad_gated, grad_own_squares))
    (
        grad_local_out,
        grad_state_in,
        grad_inner_out,
        grad_shared_c_out,
        grad_log_out,
        grad_skip_gain,
        grad_gate_z,
    ) = after_grads
    grad_final = pass_states(carry_rate, grad_state_in, -1)
    grad_carry = jnp.sum(grad_final * state_in, axis=(1, 2))
    scan_grads = pull_scan((grad_local_out, grad_carry, grad_final))
    grad_prepared = (
        scan_grads[0] + grad_inner_out,
        scan_grads[1],
        scan_grads[2] + grad_shared_c_out,
        scan_grads[3],
        scan_grads[4] + grad_log_out,
    )
    input_grads = pull_inputs(grad_prepared)
    (
        grad_mixer_ext,
        grad_shared_ext,
        grad_step_raw,
        grad_conv_main,
        grad_conv_shared,
        grad_decay_log,
        grad_dt_bias,
    ) = input_grads
    returned = passed_along((grad_mixer_ext[:lead], grad_shared_ext[:lead]), "dp", -1)
    grad_mixer_x = jnp.concatenate(
        [grad_mixer_ext[lead:-lead], grad_mixer_ext[-lead:] + returned[0]]
    )
    grad_shared_part = jnp.concatenate(
        [grad_shared_ext[lead:-lead], grad_shared_ext[-lead:] + returned[1]]
    )
    grad_query, grad_keys, grad_values = attend_back(
        queries, all_keys, all_values, block_mask(), scale, row_lse, grad_heads
    )
    grad_pairs = jnp.concatenate([grad_keys, grad_values], axis=1)
    grad_pair_own = grad_pairs[hops * group_rows :]
    for distance in range(hops, 0, -1):
        slot = hops - distance
        grad_pair_own = grad_pair_own + passed_along(
            grad_pairs[slot * group_rows : (slot + 1) * group_rows], "dp", -distance
        )
    grad_keys_own = grad_pair_own[:, :HEAD_DIMENSION]
    local_value_gradient = grad_pair_own[:, HEAD_DIMENSION:]
    grad_query_raw = rotary(grad_query, position, -1.0).reshape(group_rows, -1).astype(jnp.bfloat16)
    grad_key_raw = rotary(grad_keys_own[:, None, :], position, -1.0)[:, 0]
    key_value_gradient_full = jnp.zeros((group_rows, gathered_key_value.shape[1]), jnp.float32)
    key_value_gradient_full = lax.dynamic_update_slice_in_dim(
        key_value_gradient_full, grad_key_raw, key_value_head * HEAD_DIMENSION, 1
    )
    key_value_gradient_full = lax.dynamic_update_slice_in_dim(
        key_value_gradient_full,
        local_value_gradient,
        (KEY_VALUE_HEADS + key_value_head) * HEAD_DIMENSION,
        1,
    )
    shared = lax.psum((grad_shared_part, key_value_gradient_full), "tensor")
    bc_width = full_bc.shape[1] // tensor_size
    kv_width = gathered_key_value.shape[1] // tensor_size
    grad_bc_block = lax.dynamic_slice_in_dim(
        shared[0].astype(jnp.bfloat16), tensor_position * bc_width, bc_width, 1
    )
    grad_kv_block = lax.dynamic_slice_in_dim(
        shared[1].astype(jnp.bfloat16), tensor_position * kv_width, kv_width, 1
    )
    bc_block = lax.dynamic_slice_in_dim(full_bc, tensor_position * bc_width, bc_width, 1)
    kv_block = lax.dynamic_slice_in_dim(gathered_key_value, tensor_position * kv_width, kv_width, 1)
    grad_proj = jnp.stack([grad_gate_z, grad_mixer_x]).astype(jnp.bfloat16)
    grad_step_low = grad_step_raw.astype(jnp.bfloat16)
    grad_mamba_in = jnp.einsum("td,stc->sdc", normed, grad_proj, preferred_element_type=jnp.float32)
    grad_dt_proj = jnp.einsum(
        "td,th->dh", normed, grad_step_low, preferred_element_type=jnp.float32
    )
    grad_query_proj = jnp.einsum(
        "td,tc->dc", normed, grad_query_raw, preferred_element_type=jnp.float32
    )
    grad_bc_proj = jnp.einsum(
        "td,tc->dc", normed, grad_bc_block, preferred_element_type=jnp.float32
    )
    grad_kv_proj = jnp.einsum(
        "td,tc->dc", normed, grad_kv_block, preferred_element_type=jnp.float32
    )
    grad_normed = jnp.einsum(
        "stc,sdc->td", grad_proj, full_mamba_in, preferred_element_type=jnp.float32
    )
    grad_normed = grad_normed + jnp.einsum(
        "th,dh->td", grad_step_low, full_dt, preferred_element_type=jnp.float32
    )
    grad_normed = grad_normed + jnp.einsum(
        "tc,dc->td", grad_query_raw, full_query, preferred_element_type=jnp.float32
    )
    grad_normed = grad_normed + jnp.einsum(
        "tc,dc->td", grad_bc_block, bc_block, preferred_element_type=jnp.float32
    )
    grad_normed = grad_normed + jnp.einsum(
        "tc,dc->td", grad_kv_block, kv_block, preferred_element_type=jnp.float32
    )
    grad_normed_own = summed_rows(grad_normed)
    grad_tokens_norm, grad_norm_gain = pull_norm_one(grad_normed_own)
    grad_tokens = grad_middle + grad_tokens_norm
    late_parts = (
        grad_mamba_in[0],
        grad_mamba_in[1],
        grad_bc_proj,
        grad_kv_proj,
        grad_query_proj,
        grad_dt_proj,
    )
    early_parts = (grad_mamba_out, grad_attn_out, grad_ffn_down, grad_ffn_in[0], grad_ffn_in[1])
    early = unpack(
        lax.psum_scatter(pack(early_parts), "dp", scatter_dimension=0, tiled=True),
        [part.shape[1] for part in early_parts],
    )
    late = unpack(
        lax.psum_scatter(pack(late_parts), "dp", scatter_dimension=0, tiled=True),
        [part.shape[1] for part in late_parts],
    )
    scattered = (
        jnp.stack(late[:2]),
        late[5],
        late[2],
        late[4],
        late[3],
        early[0].T,
        early[1].T,
        jnp.stack(early[3:]),
        early[2].T,
    )

    def widen(piece, axis_at):
        new_shape = list(piece.shape)
        new_shape[axis_at] = new_shape[axis_at] * tensor_size
        return lax.dynamic_update_slice_in_dim(
            jnp.zeros(new_shape, jnp.float32),
            piece,
            tensor_position * piece.shape[axis_at],
            axis_at,
        )

    def narrow(whole, axis_at, width):
        return lax.dynamic_slice_in_dim(whole, tensor_position * width, width, axis_at)

    small = lax.psum(
        (
            grad_norm_gain,
            grad_ffn_gain,
            grad_conv_shared,
            widen(grad_conv_main, 1),
            widen(grad_decay_log, 0),
            widen(grad_dt_bias, 0),
            widen(grad_skip_gain, 0),
            widen(grad_gated_gain, 0),
        ),
        ("dp", "tensor"),
    )
    return (
        layer_out,
        grad_tokens,
        small[0],
        scattered[0],
        scattered[1],
        scattered[2],
        narrow(small[3], 1, conv_main.shape[1]),
        small[2],
        narrow(small[4], 0, local_heads),
        narrow(small[5], 0, local_heads),
        narrow(small[6], 0, local_heads),
        narrow(small[7], 0, gated_gain.shape[0]),
        scattered[5],
        scattered[3],
        scattered[4],
        scattered[6],
        small[1],
        scattered[7],
        scattered[8],
    )


def solution(mesh):
    return jax.shard_map(
        per_device,
        mesh=mesh,
        in_specs=(
            P(("dp", "tensor"), None),
            P(),
            P(),
            P(None, "dp", "tensor"),
            P("dp", "tensor"),
            P("dp", None),
            P(None, "tensor"),
            P(),
            P("tensor"),
            P("tensor"),
            P("tensor"),
            P("tensor"),
            P("tensor", "dp"),
            P("dp", "tensor"),
            P("dp", None),
            P("tensor", "dp"),
            P(),
            P(None, "dp", "tensor"),
            P("tensor", "dp"),
            P(("dp", "tensor"), None),
        ),
        out_specs=(
            P(("dp", "tensor"), None),
            P(("dp", "tensor"), None),
            P(),
            P(None, "dp", "tensor"),
            P("dp", "tensor"),
            P("dp", "tensor"),
            P(None, "tensor"),
            P(),
            P("tensor"),
            P("tensor"),
            P("tensor"),
            P("tensor"),
            P("tensor", "dp"),
            P("dp", "tensor"),
            P("dp", "tensor"),
            P("tensor", "dp"),
            P(),
            P(None, "dp", "tensor"),
            P("tensor", "dp"),
        ),
        check_vma=False,
    )
```
